128 devices in a mesh: col: 32 (over z, x, core), row: 4 (over y).
Axes of the slice: x: 4, y: 4, z: 4, core: 2. Of those that a mesh axis runs over, the one named last changes fastest.
Arguments:
- blocks: bfloat16 [16384, 128, 128], P(('col', 'row')), may hold values from -6 to 6
- dest: int32 [16384, 1], P(('col', 'row')), may hold values from 0 to 127; in each aligned block of 128 rows (0 to 127, 128 to 255, ...) at most 2 rows name the same one
- slot: int32 [16384], P(('col', 'row')), may hold values from 0 to 15
- template: bfloat16 [2048, 16384], P('row', 'col'), may hold values from -6 to 6
- kern_rows: bfloat16 [9, 31], replicated, may hold values from -1 to 1
- kern_cols: bfloat16 [9, 31], replicated, may hold values from -1 to 1
- coeffs: float32 [9, 3], replicated, may hold values from -3 to 3
Outputs:
- difference: bfloat16 [2048, 16384], P('row', 'col')
The draws below stay inside these ranges and needn't reach their ends.
Inputs may be any that keep to these rules, and one draw needn't show every extreme that they name: `dest`: among the rows of one device, at most 2 blocks name one patch, a bound that some block reaches of them.
All inputs are finite; a program needn't handle non-finite values.
Results may differ from the reference program's by a relative error of at most 0.0049.
Values may be sent and summed in bfloat16 or wider, within the bound.
No kernel may reach another device: no remote copies, remote signals or barrier semaphores. Data moves between devices by JAX's collectives and lax.ppermute only.
A program may use at most 128 MiB of HBM per device.

```python
import math
import jax
import jax.numpy as jnp
import numpy as np
from jax import lax

BASES = 9
TAPS = 31
HALF = 15
TB = 128
GRID = 4
B_DEV = 128
CAP = 2
TOTAL_BLOCKS = 16384
HEIGHT = 2048
WIDTH = 16384
N_COL = 32
N_ROW = 4
DEVICES = 128


def plant(values, own_key, low, largest):
    longest = values.shape.index(max(values.shape))
    spots = []
    for shift in (0, 1):
        where = [jax.random.randint(jax.random.fold_in(own_key, axis), (), 0, length) for axis, length in enumerate(values.shape)]
        where[longest] = (where[longest] + shift) % values.shape[longest]
        spots.append(tuple(where))
    return values.at[spots[0]].set(low).at[spots[1]].set(largest)


def shard_levels(key, extent, split, low, high):
    loudness = 1.0
    for position, shards_of in split:
        steps = jax.random.uniform(jax.random.fold_in(jax.random.fold_in(key, 6), position), (shards_of,), jnp.float32, low / len(split), high / len(split))
        loudness = loudness * jnp.repeat(jnp.exp(steps), extent[position] // shards_of).reshape((-1,) + (1,) * (len(extent) - 1 - position))
    return loudness


def rank_bounds(count, slope):
    weights = [(1 << 20) // math.isqrt(rank ** slope) + 1 for rank in range(1, count + 1)]
    spread = 1 + sum(weights) // (1 << 30)
    return np.cumsum(np.array([max(1, weight // spread) for weight in weights]))


def skewed_ids(stream_key, dims, amount, slope):
    listing = rank_bounds(amount, slope)
    lot = jax.random.randint(jax.random.fold_in(stream_key, 1), dims, 0, int(listing[amount - 1]))
    rank = jnp.searchsorted(jnp.asarray(listing, jnp.int32), lot, side="right")
    return jax.random.permutation(jax.random.fold_in(stream_key, 2), amount)[rank].astype(jnp.int32)


def deal_out(key, own, number, rows, number_of, top, most, skew):
    sequence = jax.random.permutation(key, number_of)
    packed, ordinary = load_shares(number_of, rows * top, most, skew, True), load_shares(number_of, rows * top, most, skew, False)
    places = jnp.arange(number_of)

    def named(lengths, offset_by):
        used = int((lengths > 0).sum())
        fixed = max(1, used // 4)
        shifted = fixed + (places - fixed + offset_by * (used - fixed)) % max(1, number_of - fixed)
        return jnp.zeros((number_of,), jnp.int32).at[sequence[jnp.where(places < fixed, places, shifted)]].set(jnp.asarray(lengths, jnp.int32))

    lengths = jnp.where(number % 4 == 0, named(packed, number // 4), named(ordinary, number - number // 4 - 1))
    mixed = jax.random.permutation(jax.random.fold_in(own, 3), number_of)
    giver, receiver = mixed[0:number_of // 2 * 2:2], mixed[1:number_of // 2 * 2:2]
    slack = jnp.minimum(lengths[giver] - 1, most - lengths[receiver]) // 2
    slack = jnp.where((giver == sequence[0]) | (receiver == sequence[0]) | (lengths[receiver] == 0), 0, jnp.maximum(slack, 0))
    shifted = jax.random.randint(jax.random.fold_in(own, 4), (number_of // 2,), 0, 1 << 20) % (slack + 1)
    lengths = lengths.at[giver].add(-shifted).at[receiver].add(shifted)
    members = jnp.searchsorted(jnp.cumsum(lengths), jnp.arange(rows * top), side="right").astype(jnp.int32)
    grid = members.reshape(top, rows).T
    grid = grid[jax.random.permutation(jax.random.fold_in(own, 1), rows)]
    offset_by = jax.random.randint(jax.random.fold_in(own, 2), (rows, 1), 0, top)
    return jnp.take_along_axis(grid, (jnp.arange(top)[None, :] + offset_by) % top, axis=1)


def load_shares(amount, total, bound, skew, full):
    weights = [(1 << 20) // math.isqrt(rank ** skew) + 1 for rank in range(1, amount + 1)]
    largest = bound if full else min(bound, max(-(-total // amount), total * weights[0] // sum(weights)))
    least = 1 if total - largest >= amount - 1 else 0
    holding, surplus = [largest] + [least] * (amount - 1), total - largest - least * (amount - 1)
    while surplus > 0:
        movable = [i for i in range(1, amount) if holding[i] < largest] or [i for i in range(1, amount) if holding[i] < bound]
        mass, left = sum([weights[i] for i in movable]), surplus
        for i in movable:
            addition = min(bound - holding[i], max(1, left * weights[i] // mass), surplus)
            holding[i] = holding[i] + addition
            surplus = surplus - addition
    return np.array(holding)


def noise(stream_key, dims, scale, limit, shards=(), held_as=jnp.bfloat16):
    entries = scale * jax.random.normal(stream_key, dims, jnp.float32)
    if shards:
        entries = entries * shard_levels(stream_key, dims, shards, -0.22, 0.18)
    return jnp.clip(entries, -limit, limit).astype(held_as)


def setup_inputs(seed: int = 0) -> dict:
    seeds = jax.random.split(jax.random.key(seed), 8)
    blocks = noise(seeds[0], (TOTAL_BLOCKS, TB, TB), 1.0, 6.0, ((0, 128),))
    dest_keys = jax.random.split(jax.random.fold_in(seeds[1], 1), TOTAL_BLOCKS // B_DEV)
    dest_turns = jax.random.permutation(jax.random.fold_in(seeds[1], 3), TOTAL_BLOCKS // B_DEV)
    dest = jax.vmap(lambda own, number: deal_out(jax.random.fold_in(seeds[1], 2), own, number, B_DEV, DEVICES, 1, CAP, 2))(dest_keys, dest_turns).reshape((TOTAL_BLOCKS, 1))
    slot = plant(skewed_ids(seeds[2], (TOTAL_BLOCKS,), GRID * GRID, 3), jax.random.fold_in(seeds[2], 3), 0, (GRID * GRID) - 1).astype(jnp.int32)
    template = noise(seeds[3], (HEIGHT, WIDTH), 1.0, 6.0, ((0, 4), (1, 32)))
    kern_rows = noise(seeds[4], (BASES, TAPS), 0.18, 1.0)
    kern_cols = noise(seeds[5], (BASES, TAPS), 0.18, 1.0)
    coeffs = noise(seeds[6], (BASES, 3), 0.5, 3.0, (), jnp.float32)
    return dict(blocks=blocks, dest=dest, slot=slot, template=template, kern_rows=kern_rows, kern_cols=kern_cols, coeffs=coeffs)


def reference(blocks, dest, slot, template, kern_rows, kern_cols, coeffs):
    target = dest[:, 0]
    patch_row = target % N_ROW
    patch_col = target // N_ROW
    tile_row = patch_row * GRID + slot // GRID
    tile_col = patch_col * GRID + slot % GRID
    tile_ids = (tile_row * (N_COL * GRID) + tile_col).astype(jnp.int32)
    segments = N_ROW * GRID * N_COL * GRID
    flat_blocks = blocks.astype(jnp.float32).reshape(TOTAL_BLOCKS, TB * TB)
    totals = jax.ops.segment_sum(flat_blocks, tile_ids, num_segments=segments)
    counts = jax.ops.segment_sum(jnp.ones((TOTAL_BLOCKS,), jnp.float32), tile_ids, num_segments=segments)
    tiles = totals / jnp.maximum(counts, 1.0)[:, None]
    science = tiles.reshape(N_ROW * GRID, N_COL * GRID, TB, TB).transpose(0, 2, 1, 3).reshape(HEIGHT, WIDTH)
    padded = jnp.pad(template, HALF).astype(jnp.float32)
    row_taps = kern_rows.astype(jnp.float32)
    col_taps = kern_cols.astype(jnp.float32)
    rows_pass = lax.conv_general_dilated(padded[None, None], row_taps[:, None, :, None], (1, 1), "VALID", precision=lax.Precision.HIGHEST)
    rows_pass = rows_pass.astype(jnp.bfloat16).astype(jnp.float32)
    basis_images = lax.conv_general_dilated(rows_pass, col_taps[:, None, None, :], (1, 1), "VALID", feature_group_count=BASES, precision=lax.Precision.HIGHEST)[0]
    coord_y = 2.0 * (jnp.arange(HEIGHT, dtype=jnp.float32) + 0.5) / HEIGHT - 1.0
    coord_x = 2.0 * (jnp.arange(WIDTH, dtype=jnp.float32) + 0.5) / WIDTH - 1.0
    weights = coeffs[:, 0][:, None, None] + coeffs[:, 1][:, None, None] * coord_x[None, None, :] + coeffs[:, 2][:, None, None] * coord_y[None, :, None]
    model = jnp.sum(weights * basis_images, axis=0)
    return (science - model).astype(jnp.bfloat16)
```

```python
import functools

import jax
import jax.numpy as jnp
from jax import lax
from jax.experimental import pallas as pl
from jax.experimental.pallas import tpu as pltpu
from jax.sharding import PartitionSpec as P

HALF = 15
TAPS = 31
BASES = 9
GRID = 4
TB = 128
EXTENT = GRID * TB
AXES = ("col", "row")
STEP = 2048


def edge_shift(cells, axis, up):
    count = lax.axis_size(axis)
    if up:
        pairs = [(i, i + 1) for i in range(count - 1)]
    else:
        pairs = [(i + 1, i) for i in range(count - 1)]
    return lax.ppermute(cells, axis, pairs)


def with_halo(template):
    left = edge_shift(template[:, EXTENT - HALF:], "col", True)
    right = edge_shift(template[:, :HALF], "col", False)
    wide = jnp.concatenate([left, template, right], axis=1)
    above = edge_shift(wide[EXTENT - HALF:], "row", True)
    below = edge_shift(wide[:HALF], "row", False)
    tall = jnp.concatenate([above, wide, below], axis=0)
    return jnp.pad(tall, ((0, 2), (0, 98)))


def toeplitz(taps_row):
    spread = jnp.broadcast_to(taps_row, (TB, 2 * TB))
    return pltpu.roll(spread, 0, 1, stride=1, stride_axis=0).astype(jnp.bfloat16)


def model_kernel(coeffs_ref, origin_ref, padded_ref, rows_ref, cols_ref, model_ref, band_rows, band_cols, passed):
    for b in range(BASES):
        band_rows[b] = toeplitz(rows_ref[b:b + 1, :])
        band_cols[b] = toeplitz(cols_ref[b:b + 1, :])
    height_all = float(EXTENT * 4)
    width_all = float(EXTENT * 32)

    @pl.loop(0, GRID)
    def _(q):
        source = padded_ref[pl.ds(pl.multiple_of(q * TB, TB), 160), :]

        @pl.loop(0, BASES)
        def _(b):
            passed[b] = jnp.dot(
                band_rows[b][:, :160], source, preferred_element_type=jnp.float32
            ).astype(jnp.bfloat16)

        local_y = lax.broadcasted_iota(jnp.int32, (TB, TB), 0) + q * TB
        coord_y = 2.0 * (local_y.astype(jnp.float32) + (origin_ref[0] + 0.5)) / height_all - 1.0
        for p in range(GRID):
            local_x = lax.broadcasted_iota(jnp.int32, (TB, TB), 1) + p * TB
            coord_x = 2.0 * (local_x.astype(jnp.float32) + (origin_ref[1] + 0.5)) / width_all - 1.0
            total = jnp.zeros((TB, TB), jnp.float32)
            for b in range(BASES):
                image = lax.dot_general(
                    passed[b, :, p * TB:(p + 2) * TB],
                    band_cols[b],
                    (((1,), (1,)), ((), ())),
                    preferred_element_type=jnp.float32,
                )
                weight = coeffs_ref[3 * b] + coeffs_ref[3 * b + 1] * coord_x + coeffs_ref[3 * b + 2] * coord_y
                total = total + weight * image
            model_ref[pl.ds(pl.multiple_of(q * TB, TB), TB), p * TB:(p + 1) * TB] = total


def model_of(padded, kern_rows, kern_cols, coeffs):
    taps_rows = jnp.pad(kern_rows.astype(jnp.float32), ((0, 7), (0, 2 * TB - TAPS)))
    taps_cols = jnp.pad(kern_cols.astype(jnp.float32), ((0, 7), (0, 2 * TB - TAPS)))
    origin = jnp.stack([
        lax.axis_index("row").astype(jnp.float32) * EXTENT,
        lax.axis_index("col").astype(jnp.float32) * EXTENT,
    ])
    smem = pl.BlockSpec(memory_space=pltpu.SMEM)
    vmem = pl.BlockSpec(memory_space=pltpu.VMEM)
    return pl.pallas_call(
        model_kernel,
        out_shape=jax.ShapeDtypeStruct((EXTENT, EXTENT), jnp.float32),
        in_specs=[smem, smem, vmem, vmem, vmem],
        out_specs=vmem,
        scratch_shapes=[
            pltpu.VMEM((BASES, TB, 2 * TB), jnp.bfloat16),
            pltpu.VMEM((BASES, TB, 2 * TB), jnp.bfloat16),
            pltpu.VMEM((BASES, TB, 640), jnp.bfloat16),
        ],
        compiler_params=pltpu.CompilerParams(vmem_limit_bytes=24 << 20),
        cost_estimate=pl.CostEstimate(flops=3_000_000_000, bytes_accessed=2_000_000, transcendentals=0),
    )(coeffs.reshape(-1), origin, padded, taps_rows, taps_cols)


def merge_kernel(keys_ref, high_ref, rows_ref, out_ref, acc):
    step = pl.program_id(0)

    @pl.when(step == 0)
    def _():
        acc[...] = jnp.zeros_like(acc)

    upper = rows_ref[...] * high_ref[...]
    lower = rows_ref[...] - upper
    spread = jnp.concatenate([lower, upper], axis=1)
    keys = keys_ref[0]
    marks = lax.broadcasted_iota(jnp.int32, (256, STEP), 0).astype(jnp.bfloat16)
    for part in range(4):
        wanted = (keys - float(part * 256)).astype(jnp.bfloat16)
        chosen = jnp.where(marks == wanted, jnp.bfloat16(1), jnp.bfloat16(0))
        acc[part * 256:(part + 1) * 256, :] += jnp.dot(chosen, spread, preferred_element_type=jnp.float32)

    @pl.when(step == pl.num_programs(0) - 1)
    def _():
        whole = acc[...].reshape(TB, 8, 2 * TB)
        out_ref[...] = jnp.concatenate([whole[:, :, :TB], whole[:, :, TB:]], axis=1).astype(jnp.bfloat16)


def merged(keys, rows):
    count = keys.shape[0]
    steps = count // STEP
    places = ((keys // 16) * 8 + keys % 8).astype(jnp.float32).reshape(steps, 1, STEP)
    high = jnp.broadcast_to(((keys // 8) % 2).astype(jnp.bfloat16)[:, None], (count, TB))
    return pl.pallas_call(
        merge_kernel,
        grid=(steps,),
        out_shape=jax.ShapeDtypeStruct((TB, 16, TB), jnp.bfloat16),
        in_specs=[
            pl.BlockSpec((1, 1, STEP), lambda k: (k, 0, 0)),
            pl.BlockSpec((STEP, TB), lambda k: (k, 0)),
            pl.BlockSpec((STEP, TB), lambda k: (k, 0)),
        ],
        out_specs=pl.BlockSpec((TB, 16, TB), lambda k: (0, 0, 0)),
        scratch_shapes=[pltpu.VMEM((1024, 2 * TB), jnp.float32)],
        compiler_params=pltpu.CompilerParams(vmem_limit_bytes=24 << 20),
        cost_estimate=pl.CostEstimate(flops=8_600_000_000, bytes_accessed=9_000_000, transcendentals=0),
    )(places, high, rows)


def body(blocks, dest, slot, template, kern_rows, kern_cols, coeffs):
    keys = lax.all_gather(dest[:, 0] * 16 + slot, AXES, axis=0, tiled=True)
    rows = lax.all_to_all(blocks, AXES, split_axis=1, concat_axis=0, tiled=True).reshape(-1, TB)
    model = model_of(with_halo(template), kern_rows, kern_cols, coeffs)
    mine = lax.axis_index("col") * 4 + lax.axis_index("row")
    tiles = mine * 16 + jnp.arange(16, dtype=jnp.int32)
    counts = (keys[None, :] == tiles[:, None]).astype(jnp.float32).sum(axis=1)
    inverse = 1.0 / jnp.maximum(counts, 1.0)
    sums = merged(keys, rows)
    arrived = lax.all_to_all(sums, AXES, split_axis=0, concat_axis=0, tiled=True)
    science = (
        (arrived.astype(jnp.float32) * inverse[None, :, None])
        .reshape(TB, GRID, GRID, TB)
        .transpose(1, 0, 2, 3)
        .reshape(EXTENT, EXTENT)
    )
    return (science - model).astype(jnp.bfloat16)


def solution(mesh):
    placed = (P(AXES, None, None), P(AXES, None), P(AXES), P("row", "col"), P(), P(), P())
    return jax.shard_map(body, mesh=mesh, in_specs=placed, out_specs=P("row", "col"), check_vma=False)
```

```python
import functools

import jax
import jax.numpy as jnp
from jax import lax
from jax.experimental import pallas as pl
from jax.experimental.pallas import tpu as pltpu
from jax.sharding import PartitionSpec as P

HALF = 15
TAPS = 31
BASES = 9
GRID = 4
TB = 128
EXTENT = GRID * TB
AXES = ("col", "row")
CHUNK = 16
PARTS = TB // CHUNK
DEPTH = 512
VMEM_LIMIT = 56 << 20


def edge_shift(cells, axis, up):
    count = lax.axis_size(axis)
    if up:
        pairs = [(i, i + 1) for i in range(count - 1)]
    else:
        pairs = [(i + 1, i) for i in range(count - 1)]
    return lax.ppermute(cells, axis, pairs)


def with_halo(template):
    left = edge_shift(template[:, EXTENT - HALF:], "col", True)
    right = edge_shift(template[:, :HALF], "col", False)
    wide = jnp.concatenate([left, template, right], axis=1)
    above = edge_shift(wide[EXTENT - HALF:], "row", True)
    below = edge_shift(wide[:HALF], "row", False)
    tall = jnp.concatenate([above, wide, below], axis=0)
    return jnp.pad(tall, ((0, 2), (0, 98)))


def toeplitz(taps_row):
    spread = jnp.broadcast_to(taps_row, (TB, 2 * TB))
    return pltpu.roll(spread, 0, 1, stride=1, stride_axis=0).astype(jnp.bfloat16)


def model_kernel(coeffs_ref, origin_ref, padded_ref, rows_ref, cols_ref, model_ref, band_rows, band_cols, passed):
    for b in range(BASES):
        band_rows[b] = toeplitz(rows_ref[b:b + 1, :])
        band_cols[b] = toeplitz(cols_ref[b:b + 1, :])
    height_all = float(EXTENT * 4)
    width_all = float(EXTENT * 32)

    @pl.loop(0, GRID)
    def _(q):
        source = padded_ref[pl.ds(pl.multiple_of(q * TB, TB), 160), :]

        @pl.loop(0, BASES)
        def _(b):
            passed[b] = jnp.dot(
                band_rows[b][:, :160], source, preferred_element_type=jnp.float32
            ).astype(jnp.bfloat16)

        local_y = lax.broadcasted_iota(jnp.int32, (TB, TB), 0) + q * TB
        coord_y = 2.0 * (local_y.astype(jnp.float32) + (origin_ref[0] + 0.5)) / height_all - 1.0
        for p in range(GRID):
            local_x = lax.broadcasted_iota(jnp.int32, (TB, TB), 1) + p * TB
            coord_x = 2.0 * (local_x.astype(jnp.float32) + (origin_ref[1] + 0.5)) / width_all - 1.0
            total = jnp.zeros((TB, TB), jnp.float32)
            for b in range(BASES):
                image = lax.dot_general(
                    passed[b, :, p * TB:(p + 2) * TB],
                    band_cols[b],
                    (((1,), (1,)), ((), ())),
                    preferred_element_type=jnp.float32,
                )
                weight = coeffs_ref[3 * b] + coeffs_ref[3 * b + 1] * coord_x + coeffs_ref[3 * b + 2] * coord_y
                total = total + weight * image
            model_ref[pl.ds(pl.multiple_of(q * TB, TB), TB), p * TB:(p + 1) * TB] = total


def model_of(padded, kern_rows, kern_cols, coeffs):
    taps_rows = jnp.pad(kern_rows.astype(jnp.float32), ((0, 7), (0, 2 * TB - TAPS)))
    taps_cols = jnp.pad(kern_cols.astype(jnp.float32), ((0, 7), (0, 2 * TB - TAPS)))
    origin = jnp.stack([
        lax.axis_index("row").astype(jnp.float32) * EXTENT,
        lax.axis_index("col").astype(jnp.float32) * EXTENT,
    ])
    smem = pl.BlockSpec(memory_space=pltpu.SMEM)
    vmem = pl.BlockSpec(memory_space=pltpu.VMEM)
    return pl.pallas_call(
        model_kernel,
        out_shape=jax.ShapeDtypeStruct((EXTENT, EXTENT), jnp.float32),
        in_specs=[smem, smem, vmem, vmem, vmem],
        out_specs=vmem,
        scratch_shapes=[
            pltpu.VMEM((BASES, TB, 2 * TB), jnp.bfloat16),
            pltpu.VMEM((BASES, TB, 2 * TB), jnp.bfloat16),
            pltpu.VMEM((BASES, TB, 640), jnp.bfloat16),
        ],
        compiler_params=pltpu.CompilerParams(vmem_limit_bytes=24 << 20),
        cost_estimate=pl.CostEstimate(flops=3_000_000_000, bytes_accessed=2_000_000, transcendentals=0),
    )(coeffs.reshape(-1), origin, padded, taps_rows, taps_cols)


def turn_kernel(dest_ref, slot_ref, blocks_ref, out_ref, loaded, swapped, ready, arriving, leaving):
    arrivals = []
    for k in range(PARTS):
        part = pl.ds(k * CHUNK, CHUNK)
        arrivals.append(pltpu.make_async_copy(blocks_ref.at[part], loaded.at[part], arriving.at[k]))
        arrivals[k].start()
    dests = dest_ref[...].astype(jnp.float32)
    slots = slot_ref[...].astype(jnp.float32)
    ranked = dests * float(TB) + lax.broadcasted_iota(jnp.int32, (1, TB), 1).astype(jnp.float32)
    across = jnp.broadcast_to(ranked, (TB, TB))
    place = jnp.where(across.T < across, 1.0, 0.0).sum(axis=0, keepdims=True)
    down = lax.broadcasted_iota(jnp.int32, (TB, TB), 0).astype(jnp.float32)
    order = jnp.where(down == place, 1.0, 0.0).astype(jnp.bfloat16)
    pair = jnp.concatenate([dests, slots, jnp.zeros((14, TB), jnp.float32)], axis=0).astype(jnp.bfloat16)
    labels = lax.dot_general(
        pair, order, (((1,), (1,)), ((), ())), preferred_element_type=jnp.float32
    ).astype(jnp.bfloat16)[:8]
    for k in range(PARTS):
        arrivals[k].wait()
        part = pl.ds(k * CHUNK, CHUNK)
        swapped[:, part, :] = jnp.swapaxes(loaded[part], 0, 1)
    departures = []
    for k in range(PARTS):
        for r in range(k * CHUNK, (k + 1) * CHUNK):
            ready[r, :TB, :] = jnp.dot(
                order, swapped[r], preferred_element_type=jnp.float32
            ).astype(jnp.bfloat16)
            ready[r, TB:, :] = labels
        part = pl.ds(k * CHUNK, CHUNK)
        departures.append(pltpu.make_async_copy(ready.at[part], out_ref.at[part], leaving.at[k]))
        departures[k].start()
    for k in range(PARTS):
        departures[k].wait()


def turned(blocks, dest, slot):
    label = pl.BlockSpec(memory_space=pltpu.VMEM)
    far = pl.BlockSpec(memory_space=pl.ANY)
    return pl.pallas_call(
        turn_kernel,
        out_shape=jax.ShapeDtypeStruct((TB, TB + 8, TB), jnp.bfloat16),
        in_specs=[label, label, far],
        out_specs=far,
        scratch_shapes=[
            pltpu.VMEM((TB, TB, TB), jnp.bfloat16),
            pltpu.VMEM((TB, TB, TB), jnp.bfloat16),
            pltpu.VMEM((TB, TB + 8, TB), jnp.bfloat16),
            pltpu.SemaphoreType.DMA((PARTS,)),
            pltpu.SemaphoreType.DMA((PARTS,)),
        ],
        compiler_params=pltpu.CompilerParams(vmem_limit_bytes=VMEM_LIMIT),
        cost_estimate=pl.CostEstimate(flops=600_000_000, bytes_accessed=8_700_000, transcendentals=0),
    )(dest.reshape(1, TB), slot.reshape(1, TB), blocks)


def merge_kernel(arrived_ref, out_ref, keys_ref, labels, rows, acc, spread, labels_sem, rows_sem):
    named = pltpu.make_async_copy(arrived_ref.at[:, pl.ds(TB, 8), :], labels, labels_sem)
    named.start()
    arrivals = []
    for k in range(PARTS):
        part = pl.ds(k * CHUNK, CHUNK)
        arrivals.append(pltpu.make_async_copy(arrived_ref.at[:, part, :], rows.at[k], rows_sem.at[k]))
        arrivals[k].start()
    acc[...] = jnp.zeros_like(acc)
    lanes = lax.broadcasted_iota(jnp.int32, (TB, TB), 1) // CHUNK
    owners = lax.broadcasted_iota(jnp.int32, (TB, TB), 0) % 8
    named.wait()
    tags = labels[...].astype(jnp.float32)
    keys = tags[:, 0, :] * 16.0 + tags[:, 1, :]
    keys_ref[...] = keys
    skewed = pltpu.roll(keys, 0, 1, stride=CHUNK, stride_axis=0)
    for k in range(PARTS):
        shifted = pltpu.roll(skewed, (TB - k * CHUNK) % TB, 1)
        lines = jnp.where(lanes == owners, shifted, 0.0).reshape(16, 8, TB).sum(axis=1)
        dests = jnp.floor(lines * (1.0 / 16.0))
        slots = lines - 16.0 * dests
        high = jnp.where(slots >= 8.0, 1.0, 0.0)
        places = dests * 8.0 + slots - 8.0 * high - float(k * 64)
        high_down = high.T
        arrivals[k].wait()
        for g in range(16):
            taken = rows[k, g * 8:(g + 1) * 8].reshape(TB, TB)
            mask = jnp.broadcast_to(high_down[:, g:g + 1], (TB, TB)).astype(jnp.bfloat16)
            upper = taken * mask
            spread[k % 2, g * TB:(g + 1) * TB, TB:] = upper
            spread[k % 2, g * TB:(g + 1) * TB, :TB] = taken - upper
        line = jnp.concatenate([places[g:g + 1, :] for g in range(16)], axis=1)
        for first, size in ((0, 256), (256, 256), (512, 64)):
            marks = lax.broadcasted_iota(jnp.int32, (size, DEPTH), 0).astype(jnp.bfloat16)
            wanted = (line - float(first)).astype(jnp.bfloat16)
            total = acc[k * 64 + first:k * 64 + first + size, :]
            for q in range(0, 16 * TB, DEPTH):
                chosen = jnp.where(marks == wanted[:, q:q + DEPTH], jnp.bfloat16(1), jnp.bfloat16(0))
                total = total + jnp.dot(chosen, spread[k % 2, q:q + DEPTH, :], preferred_element_type=jnp.float32)
            acc[k * 64 + first:k * 64 + first + size, :] = total
    whole = acc[...].reshape(TB, 8, 2 * TB)
    out_ref[...] = jnp.concatenate([whole[:, :, :TB], whole[:, :, TB:]], axis=1).astype(jnp.bfloat16)


def merged(arrived):
    near = pl.BlockSpec(memory_space=pltpu.VMEM)
    return pl.pallas_call(
        merge_kernel,
        out_shape=(
            jax.ShapeDtypeStruct((TB, 16, TB), jnp.bfloat16),
            jax.ShapeDtypeStruct((TB, TB), jnp.float32),
        ),
        in_specs=[pl.BlockSpec(memory_space=pl.ANY)],
        out_specs=(near, near),
        scratch_shapes=[
            pltpu.VMEM((TB, 8, TB), jnp.bfloat16),
            pltpu.VMEM((PARTS, TB, CHUNK, TB), jnp.bfloat16),
            pltpu.VMEM((1024, 2 * TB), jnp.float32),
            pltpu.VMEM((2, 16 * TB, 2 * TB), jnp.bfloat16),
            pltpu.SemaphoreType.DMA,
            pltpu.SemaphoreType.DMA((PARTS,)),
        ],
        compiler_params=pltpu.CompilerParams(vmem_limit_bytes=VMEM_LIMIT),
        cost_estimate=pl.CostEstimate(flops=5_000_000_000, bytes_accessed=5_000_000, transcendentals=0),
    )(arrived)


def body(blocks, dest, slot, template, kern_rows, kern_cols, coeffs):
    parcels = turned(blocks, dest, slot)
    arrived = lax.all_to_all(parcels, AXES, split_axis=0, concat_axis=0, tiled=True)
    model = model_of(with_halo(template), kern_rows, kern_cols, coeffs)
    sums, keys = merged(arrived)
    gathered = lax.all_to_all(sums, AXES, split_axis=0, concat_axis=0, tiled=True)
    mine = lax.axis_index("col") * 4 + lax.axis_index("row")
    tiles = (mine * 16 + jnp.arange(16, dtype=jnp.int32)).astype(jnp.float32)
    counts = (keys[None] == tiles[:, None, None]).astype(jnp.float32).sum(axis=(1, 2))
    inverse = 1.0 / jnp.maximum(counts, 1.0)
    science = (
        (gathered.astype(jnp.float32) * inverse[None, :, None])
        .reshape(TB, GRID, GRID, TB)
        .transpose(1, 0, 2, 3)
        .reshape(EXTENT, EXTENT)
    )
    return (science - model).astype(jnp.bfloat16)


def solution(mesh):
    placed = (P(AXES, None, None), P(AXES, None), P(AXES), P("row", "col"), P(), P(), P())
    return jax.shard_map(body, mesh=mesh, in_specs=placed, out_specs=P("row", "col"), check_vma=False)
```

```python
import functools

import jax
import jax.numpy as jnp
from jax import lax
from jax.experimental import pallas as pl
from jax.experimental.pallas import tpu as pltpu
from jax.sharding import PartitionSpec as P

HALF = 15
TAPS = 31
BASES = 9
GRID = 4
TB = 128
EXTENT = GRID * TB
AXES = ("col", "row")
CHUNK = 16
PARTS = TB // CHUNK
DEPTH = 512
VMEM_LIMIT = 56 << 20


def edge_shift(cells, axis, up):
    count = lax.axis_size(axis)
    if up:
        pairs = [(i, i + 1) for i in range(count - 1)]
    else:
        pairs = [(i + 1, i) for i in range(count - 1)]
    return lax.ppermute(cells, axis, pairs)


def with_halo(template):
    left = edge_shift(template[:, EXTENT - HALF:], "col", True)
    right = edge_shift(template[:, :HALF], "col", False)
    wide = jnp.concatenate([left, template, right], axis=1)
    above = edge_shift(wide[EXTENT - HALF:], "row", True)
    below = edge_shift(wide[:HALF], "row", False)
    tall = jnp.concatenate([above, wide, below], axis=0)
    return jnp.pad(tall, ((0, 2), (0, 98)))


def toeplitz(taps_row):
    spread = jnp.broadcast_to(taps_row, (TB, 2 * TB))
    return pltpu.roll(spread, 0, 1, stride=1, stride_axis=0).astype(jnp.bfloat16)


def model_kernel(coeffs_ref, origin_ref, padded_ref, rows_ref, cols_ref, model_ref, band_rows, band_cols, passed):
    for b in range(BASES):
        band_rows[b] = toeplitz(rows_ref[b:b + 1, :])
        band_cols[b] = toeplitz(cols_ref[b:b + 1, :])
    height_all = float(EXTENT * 4)
    width_all = float(EXTENT * 32)

    @pl.loop(0, GRID)
    def _(q):
        source = padded_ref[pl.ds(pl.multiple_of(q * TB, TB), 160), :]

        @pl.loop(0, BASES)
        def _(b):
            passed[b] = jnp.dot(
                band_rows[b][:, :160], source, preferred_element_type=jnp.float32
            ).astype(jnp.bfloat16)

        local_y = lax.broadcasted_iota(jnp.int32, (TB, TB), 0) + q * TB
        coord_y = 2.0 * (local_y.astype(jnp.float32) + (origin_ref[0] + 0.5)) / height_all - 1.0
        for p in range(GRID):
            local_x = lax.broadcasted_iota(jnp.int32, (TB, TB), 1) + p * TB
            coord_x = 2.0 * (local_x.astype(jnp.float32) + (origin_ref[1] + 0.5)) / width_all - 1.0
            total = jnp.zeros((TB, TB), jnp.float32)
            for b in range(BASES):
                image = lax.dot_general(
                    passed[b, :, p * TB:(p + 2) * TB],
                    band_cols[b],
                    (((1,), (1,)), ((), ())),
                    preferred_element_type=jnp.float32,
                )
                weight = coeffs_ref[3 * b] + coeffs_ref[3 * b + 1] * coord_x + coeffs_ref[3 * b + 2] * coord_y
                total = total + weight * image
            model_ref[pl.ds(pl.multiple_of(q * TB, TB), TB), p * TB:(p + 1) * TB] = total


def model_of(padded, kern_rows, kern_cols, coeffs):
    taps_rows = jnp.pad(kern_rows.astype(jnp.float32), ((0, 7), (0, 2 * TB - TAPS)))
    taps_cols = jnp.pad(kern_cols.astype(jnp.float32), ((0, 7), (0, 2 * TB - TAPS)))
    origin = jnp.stack([
        lax.axis_index("row").astype(jnp.float32) * EXTENT,
        lax.axis_index("col").astype(jnp.float32) * EXTENT,
    ])
    smem = pl.BlockSpec(memory_space=pltpu.SMEM)
    vmem = pl.BlockSpec(memory_space=pltpu.VMEM)
    return pl.pallas_call(
        model_kernel,
        out_shape=jax.ShapeDtypeStruct((EXTENT, EXTENT), jnp.float32),
        in_specs=[smem, smem, vmem, vmem, vmem],
        out_specs=vmem,
        scratch_shapes=[
            pltpu.VMEM((BASES, TB, 2 * TB), jnp.bfloat16),
            pltpu.VMEM((BASES, TB, 2 * TB), jnp.bfloat16),
            pltpu.VMEM((BASES, TB, 640), jnp.bfloat16),
        ],
        compiler_params=pltpu.CompilerParams(vmem_limit_bytes=24 << 20),
        cost_estimate=pl.CostEstimate(flops=3_000_000_000, bytes_accessed=2_000_000, transcendentals=0),
    )(coeffs.reshape(-1), origin, padded, taps_rows, taps_cols)


def turn_kernel(dest_ref, slot_ref, blocks_ref, out_ref, loaded, swapped, ready, arriving, leaving):
    arrivals = []
    for k in range(PARTS):
        part = pl.ds(k * CHUNK, CHUNK)
        arrivals.append(pltpu.make_async_copy(blocks_ref.at[part], loaded.at[part], arriving.at[k]))
        arrivals[k].start()
    dests = dest_ref[...].astype(jnp.float32)
    slots = slot_ref[...].astype(jnp.float32)
    ranked = dests * float(TB) + lax.broadcasted_iota(jnp.int32, (1, TB), 1).astype(jnp.float32)
    across = jnp.broadcast_to(ranked, (TB, TB))
    place = jnp.where(across.T < across, 1.0, 0.0).sum(axis=0, keepdims=True)
    down = lax.broadcasted_iota(jnp.int32, (TB, TB), 0).astype(jnp.float32)
    order = jnp.where(down == place, 1.0, 0.0).astype(jnp.bfloat16)
    pair = jnp.concatenate([dests, slots, jnp.zeros((14, TB), jnp.float32)], axis=0).astype(jnp.bfloat16)
    labels = lax.dot_general(
        pair, order, (((1,), (1,)), ((), ())), preferred_element_type=jnp.float32
    ).astype(jnp.bfloat16)[:8]
    for k in range(PARTS):
        arrivals[k].wait()
        part = pl.ds(k * CHUNK, CHUNK)
        swapped[:, part, :] = jnp.swapaxes(loaded[part], 0, 1)
    departures = []
    for k in range(PARTS):
        for r in range(k * CHUNK, (k + 1) * CHUNK):
            ready[r, :TB, :] = jnp.dot(
                order, swapped[r], preferred_element_type=jnp.float32
            ).astype(jnp.bfloat16)
            ready[r, TB:, :] = labels
        part = pl.ds(k * CHUNK, CHUNK)
        departures.append(pltpu.make_async_copy(ready.at[part], out_ref.at[part], leaving.at[k]))
        departures[k].start()
    for k in range(PARTS):
        departures[k].wait()


def turned(blocks, dest, slot):
    label = pl.BlockSpec(memory_space=pltpu.VMEM)
    far = pl.BlockSpec(memory_space=pl.ANY)
    return pl.pallas_call(
        turn_kernel,
        out_shape=jax.ShapeDtypeStruct((TB, TB + 8, TB), jnp.bfloat16),
        in_specs=[label, label, far],
        out_specs=far,
        scratch_shapes=[
            pltpu.VMEM((TB, TB, TB), jnp.bfloat16),
            pltpu.VMEM((TB, TB, TB), jnp.bfloat16),
            pltpu.VMEM((TB, TB + 8, TB), jnp.bfloat16),
            pltpu.SemaphoreType.DMA((PARTS,)),
            pltpu.SemaphoreType.DMA((PARTS,)),
        ],
        compiler_params=pltpu.CompilerParams(vmem_limit_bytes=VMEM_LIMIT),
        cost_estimate=pl.CostEstimate(flops=600_000_000, bytes_accessed=8_700_000, transcendentals=0),
    )(dest.reshape(1, TB), slot.reshape(1, TB), blocks)


def merge_kernel(arrived_ref, out_ref, keys_ref, labels, rows, acc, spread, labels_sem, rows_sem):
    named = pltpu.make_async_copy(arrived_ref.at[:, pl.ds(TB, 8), :], labels, labels_sem)
    named.start()
    arrivals = []
    for k in range(PARTS):
        part = pl.ds(k * CHUNK, CHUNK)
        arrivals.append(pltpu.make_async_copy(arrived_ref.at[:, part, :], rows.at[k], rows_sem.at[k]))
        arrivals[k].start()
    acc[...] = jnp.zeros_like(acc)
    lanes = lax.broadcasted_iota(jnp.int32, (TB, TB), 1) // CHUNK
    owners = lax.broadcasted_iota(jnp.int32, (TB, TB), 0) % 8
    named.wait()
    tags = labels[...].astype(jnp.float32)
    keys = tags[:, 0, :] * 16.0 + tags[:, 1, :]
    keys_ref[...] = keys
    skewed = pltpu.roll(keys, 0, 1, stride=CHUNK, stride_axis=0)
    for k in range(PARTS):
        arrivals[k].wait()
    for k in range(PARTS):
        shifted = pltpu.roll(skewed, (TB - k * CHUNK) % TB, 1)
        lines = jnp.where(lanes == owners, shifted, 0.0).reshape(16, 8, TB).sum(axis=1)
        dests = jnp.floor(lines * (1.0 / 16.0))
        slots = lines - 16.0 * dests
        high = jnp.where(slots >= 8.0, 1.0, 0.0)
        places = dests * 8.0 + slots - 8.0 * high - float(k * 64)
        high_down = high.T
        for g in range(16):
            taken = rows[k, g * 8:(g + 1) * 8].reshape(TB, TB)
            mask = jnp.broadcast_to(high_down[:, g:g + 1], (TB, TB)).astype(jnp.bfloat16)
            upper = taken * mask
            spread[k % 2, g * TB:(g + 1) * TB, TB:] = upper
            spread[k % 2, g * TB:(g + 1) * TB, :TB] = taken - upper
        line = jnp.concatenate([places[g:g + 1, :] for g in range(16)], axis=1)
        for first, size in ((0, 256), (256, 320)):
            middle = size // 2
            marks = (lax.broadcasted_iota(jnp.int32, (size, DEPTH), 0) - middle).astype(jnp.bfloat16)
            wanted = (line - float(first + middle)).astype(jnp.bfloat16)
            window = slice(k * 64 + first, k * 64 + first + size)
            total = acc[window, :]
            for q in range(0, 16 * TB, DEPTH):
                chosen = jnp.where(marks == wanted[:, q:q + DEPTH], jnp.bfloat16(1), jnp.bfloat16(0))
                total = total + jnp.dot(chosen, spread[k % 2, q:q + DEPTH, :], preferred_element_type=jnp.float32)
            acc[window, :] = total
    whole = acc[...].reshape(TB, 8, 2 * TB)
    out_ref[...] = jnp.concatenate([whole[:, :, :TB], whole[:, :, TB:]], axis=1).astype(jnp.bfloat16)


def merged(arrived):
    near = pl.BlockSpec(memory_space=pltpu.VMEM)
    return pl.pallas_call(
        merge_kernel,
        out_shape=(
            jax.ShapeDtypeStruct((TB, 16, TB), jnp.bfloat16),
            jax.ShapeDtypeStruct((TB, TB), jnp.float32),
        ),
        in_specs=[pl.BlockSpec(memory_space=pl.ANY)],
        out_specs=(near, near),
        scratch_shapes=[
            pltpu.VMEM((TB, 8, TB), jnp.bfloat16),
            pltpu.VMEM((PARTS, TB, CHUNK, TB), jnp.bfloat16),
            pltpu.VMEM((1024, 2 * TB), jnp.float32),
            pltpu.VMEM((2, 16 * TB, 2 * TB), jnp.bfloat16),
            pltpu.SemaphoreType.DMA,
            pltpu.SemaphoreType.DMA((PARTS,)),
        ],
        compiler_params=pltpu.CompilerParams(vmem_limit_bytes=VMEM_LIMIT),
        cost_estimate=pl.CostEstimate(flops=5_000_000_000, bytes_accessed=5_000_000, transcendentals=0),
    )(arrived)


def body(blocks, dest, slot, template, kern_rows, kern_cols, coeffs):
    parcels = turned(blocks, dest, slot)
    arrived = lax.all_to_all(parcels, AXES, split_axis=0, concat_axis=0, tiled=True)
    model = model_of(with_halo(template), kern_rows, kern_cols, coeffs)
    sums, keys = merged(arrived)
    gathered = lax.all_to_all(sums, AXES, split_axis=0, concat_axis=0, tiled=True)
    mine = lax.axis_index("col") * 4 + lax.axis_index("row")
    tiles = (mine * 16 + jnp.arange(16, dtype=jnp.int32)).astype(jnp.float32)
    counts = (keys[None] == tiles[:, None, None]).astype(jnp.float32).sum(axis=(1, 2))
    inverse = 1.0 / jnp.maximum(counts, 1.0)
    science = (
        (gathered.astype(jnp.float32) * inverse[None, :, None])
        .reshape(TB, GRID, GRID, TB)
        .transpose(1, 0, 2, 3)
        .reshape(EXTENT, EXTENT)
    )
    return (science - model).astype(jnp.bfloat16)


def solution(mesh):
    placed = (P(AXES, None, None), P(AXES, None), P(AXES), P("row", "col"), P(), P(), P())
    return jax.shard_map(body, mesh=mesh, in_specs=placed, out_specs=P("row", "col"), check_vma=False)
```

```python
import functools

import jax
import jax.numpy as jnp
from jax import lax
from jax.experimental import pallas as pl
from jax.experimental.pallas import tpu as pltpu
from jax.sharding import PartitionSpec as P

HALF = 15
TAPS = 31
BASES = 9
GRID = 4
TB = 128
EXTENT = GRID * TB
AXES = ("col", "row")
CHUNK = 16
PARTS = TB // CHUNK
DEPTH = 512
VMEM_LIMIT = 56 << 20


def edge_shift(cells, axis, up):
    count = lax.axis_size(axis)
    if up:
        pairs = [(i, i + 1) for i in range(count - 1)]
    else:
        pairs = [(i + 1, i) for i in range(count - 1)]
    return lax.ppermute(cells, axis, pairs)


def with_halo(template, blank):
    left = edge_shift(template[:, EXTENT - HALF:], "col", True)
    right = edge_shift(template[:, :HALF], "col", False)
    wide = jnp.concatenate([left, template, right], axis=1)
    above = edge_shift(wide[EXTENT - HALF:], "row", True)
    below = edge_shift(wide[:HALF], "row", False)
    tall = jnp.concatenate([above, wide, below], axis=0)
    return (jnp.pad(tall, ((0, 2), (0, 98))).astype(jnp.float32) + blank).astype(jnp.bfloat16)


def toeplitz(taps_row):
    spread = jnp.broadcast_to(taps_row, (TB, 2 * TB))
    return pltpu.roll(spread, 0, 1, stride=1, stride_axis=0).astype(jnp.bfloat16)


def model_kernel(coeffs_ref, origin_ref, padded_ref, rows_ref, cols_ref, model_ref, band_rows, band_cols, passed):
    for b in range(BASES):
        band_rows[b * TB:(b + 1) * TB, :] = toeplitz(rows_ref[b:b + 1, :])
        band_cols[b] = toeplitz(cols_ref[b:b + 1, :])
    height_all = float(EXTENT * 4)
    width_all = float(EXTENT * 32)
    for q in range(GRID):
        stacked = jnp.dot(
            band_rows[:, :160], padded_ref[q * TB:q * TB + 160, :], preferred_element_type=jnp.float32
        ).astype(jnp.bfloat16)
        for b in range(BASES):
            passed[b, q * TB:(q + 1) * TB, :] = stacked[b * TB:(b + 1) * TB, :]
    local_y = lax.broadcasted_iota(jnp.int32, (EXTENT, TB), 0)
    coord_y = 2.0 * (local_y.astype(jnp.float32) + (origin_ref[0] + 0.5)) / height_all - 1.0
    for p in range(GRID):
        local_x = lax.broadcasted_iota(jnp.int32, (1, TB), 1) + p * TB
        coord_x = 2.0 * (local_x.astype(jnp.float32) + (origin_ref[1] + 0.5)) / width_all - 1.0
        total = jnp.zeros((EXTENT, TB), jnp.float32)
        for b in range(BASES):
            image = lax.dot_general(
                passed[b, :, p * TB:(p + 2) * TB],
                band_cols[b],
                (((1,), (1,)), ((), ())),
                preferred_element_type=jnp.float32,
            )
            weight = (coeffs_ref[3 * b] + coeffs_ref[3 * b + 1] * coord_x) + coeffs_ref[3 * b + 2] * coord_y
            total = total + weight * image
        model_ref[:, p * TB:(p + 1) * TB] = total


def model_of(padded, kern_rows, kern_cols, coeffs):
    taps_rows = jnp.pad(kern_rows.astype(jnp.float32), ((0, 7), (0, 2 * TB - TAPS)))
    taps_cols = jnp.pad(kern_cols.astype(jnp.float32), ((0, 7), (0, 2 * TB - TAPS)))
    origin = jnp.stack([
        lax.axis_index("row").astype(jnp.float32) * EXTENT,
        lax.axis_index("col").astype(jnp.float32) * EXTENT,
    ])
    smem = pl.BlockSpec(memory_space=pltpu.SMEM)
    vmem = pl.BlockSpec(memory_space=pltpu.VMEM)
    return pl.pallas_call(
        model_kernel,
        out_shape=jax.ShapeDtypeStruct((EXTENT, EXTENT), jnp.float32),
        in_specs=[smem, smem, vmem, vmem, vmem],
        out_specs=vmem,
        scratch_shapes=[
            pltpu.VMEM((BASES * TB, 2 * TB), jnp.bfloat16),
            pltpu.VMEM((BASES, TB, 2 * TB), jnp.bfloat16),
            pltpu.VMEM((BASES, EXTENT, 640), jnp.bfloat16),
        ],
        compiler_params=pltpu.CompilerParams(vmem_limit_bytes=32 << 20),
        cost_estimate=pl.CostEstimate(flops=3_000_000_000, bytes_accessed=2_000_000, transcendentals=0),
    )(coeffs.reshape(-1), origin, padded, taps_rows, taps_cols)


def turn_kernel(dest_ref, slot_ref, blocks_ref, out_ref, loaded, swapped, ready, arriving, leaving):
    arrivals = []
    for k in range(PARTS):
        part = pl.ds(k * CHUNK, CHUNK)
        arrivals.append(pltpu.make_async_copy(blocks_ref.at[part], loaded.at[part], arriving.at[k]))
        arrivals[k].start()
    dests = dest_ref[...].astype(jnp.float32)
    slots = slot_ref[...].astype(jnp.float32)
    ranked = dests * float(TB) + lax.broadcasted_iota(jnp.int32, (1, TB), 1).astype(jnp.float32)
    across = jnp.broadcast_to(ranked, (TB, TB))
    place = jnp.where(across.T < across, 1.0, 0.0).sum(axis=0, keepdims=True)
    down = lax.broadcasted_iota(jnp.int32, (TB, TB), 0).astype(jnp.float32)
    order = jnp.where(down == place, 1.0, 0.0).astype(jnp.bfloat16)
    pair = jnp.concatenate([dests, slots, jnp.zeros((14, TB), jnp.float32)], axis=0).astype(jnp.bfloat16)
    labels = lax.dot_general(
        pair, order, (((1,), (1,)), ((), ())), preferred_element_type=jnp.float32
    ).astype(jnp.bfloat16)[:8]
    for k in range(PARTS):
        arrivals[k].wait()
        part = pl.ds(k * CHUNK, CHUNK)
        swapped[:, part, :] = jnp.swapaxes(loaded[part], 0, 1)
    departures = []
    for k in range(PARTS):
        for r in range(k * CHUNK, (k + 1) * CHUNK):
            ready[r, :TB, :] = jnp.dot(
                order, swapped[r], preferred_element_type=jnp.float32
            ).astype(jnp.bfloat16)
            ready[r, TB:, :] = labels
        part = pl.ds(k * CHUNK, CHUNK)
        departures.append(pltpu.make_async_copy(ready.at[part], out_ref.at[part], leaving.at[k]))
        departures[k].start()
    for k in range(PARTS):
        departures[k].wait()


def turned(blocks, dest, slot):
    label = pl.BlockSpec(memory_space=pltpu.VMEM)
    far = pl.BlockSpec(memory_space=pl.ANY)
    return pl.pallas_call(
        turn_kernel,
        out_shape=jax.ShapeDtypeStruct((TB, TB + 8, TB), jnp.bfloat16),
        in_specs=[label, label, far],
        out_specs=far,
        scratch_shapes=[
            pltpu.VMEM((TB, TB, TB), jnp.bfloat16),
            pltpu.VMEM((TB, TB, TB), jnp.bfloat16),
            pltpu.VMEM((TB, TB + 8, TB), jnp.bfloat16),
            pltpu.SemaphoreType.DMA((PARTS,)),
            pltpu.SemaphoreType.DMA((PARTS,)),
        ],
        compiler_params=pltpu.CompilerParams(vmem_limit_bytes=VMEM_LIMIT),
        cost_estimate=pl.CostEstimate(flops=600_000_000, bytes_accessed=8_700_000, transcendentals=0),
    )(dest.reshape(1, TB), slot.reshape(1, TB), blocks)


def merge_kernel(arrived_ref, out_ref, keys_ref, blank_ref, labels, rows, acc, spread, labels_sem, rows_sem):
    named = pltpu.make_async_copy(arrived_ref.at[:, pl.ds(TB, 8), :], labels, labels_sem)
    named.start()
    arrivals = []
    for k in range(PARTS):
        part = pl.ds(k * CHUNK, CHUNK)
        arrivals.append(pltpu.make_async_copy(arrived_ref.at[:, part, :], rows.at[k], rows_sem.at[k]))
        arrivals[k].start()
    acc[...] = jnp.zeros_like(acc)
    lanes = lax.broadcasted_iota(jnp.int32, (TB, TB), 1) // CHUNK
    owners = lax.broadcasted_iota(jnp.int32, (TB, TB), 0) % 8
    named.wait()
    tags = labels[...].astype(jnp.float32)
    keys = tags[:, 0, :] * 16.0 + tags[:, 1, :]
    keys_ref[...] = keys
    blank_ref[...] = jnp.zeros_like(blank_ref)
    skewed = pltpu.roll(keys, 0, 1, stride=CHUNK, stride_axis=0)
    for k in range(PARTS):
        arrivals[k].wait()
    for k in range(PARTS):
        shifted = pltpu.roll(skewed, (TB - k * CHUNK) % TB, 1)
        lines = jnp.where(lanes == owners, shifted, 0.0).reshape(16, 8, TB).sum(axis=1)
        dests = jnp.floor(lines * (1.0 / 16.0))
        slots = lines - 16.0 * dests
        high = jnp.where(slots >= 8.0, 1.0, 0.0)
        places = dests * 8.0 + slots - 8.0 * high - float(k * 64)
        high_down = high.T
        for g in range(16):
            taken = rows[k, g * 8:(g + 1) * 8].reshape(TB, TB)
            mask = jnp.broadcast_to(high_down[:, g:g + 1], (TB, TB)).astype(jnp.bfloat16)
            upper = taken * mask
            spread[k % 2, g * TB:(g + 1) * TB, TB:] = upper
            spread[k % 2, g * TB:(g + 1) * TB, :TB] = taken - upper
        line = jnp.concatenate([places[g:g + 1, :] for g in range(16)], axis=1)
        for first, size in ((0, 256), (256, 320)):
            middle = size // 2
            marks = (lax.broadcasted_iota(jnp.int32, (size, DEPTH), 0) - middle).astype(jnp.bfloat16)
            wanted = (line - float(first + middle)).astype(jnp.bfloat16)
            window = slice(k * 64 + first, k * 64 + first + size)
            total = acc[window, :]
            for q in range(0, 16 * TB, DEPTH):
                chosen = jnp.where(marks == wanted[:, q:q + DEPTH], jnp.bfloat16(1), jnp.bfloat16(0))
                total = total + jnp.dot(chosen, spread[k % 2, q:q + DEPTH, :], preferred_element_type=jnp.float32)
            acc[window, :] = total
    whole = acc[...].reshape(TB, 8, 2 * TB)
    out_ref[...] = jnp.concatenate([whole[:, :, :TB], whole[:, :, TB:]], axis=1).astype(jnp.bfloat16)


def merged(arrived):
    near = pl.BlockSpec(memory_space=pltpu.VMEM)
    return pl.pallas_call(
        merge_kernel,
        out_shape=(
            jax.ShapeDtypeStruct((TB, 16, TB), jnp.bfloat16),
            jax.ShapeDtypeStruct((TB, TB), jnp.float32),
            jax.ShapeDtypeStruct((1, 640), jnp.float32),
        ),
        in_specs=[pl.BlockSpec(memory_space=pl.ANY)],
        out_specs=(near, near, near),
        scratch_shapes=[
            pltpu.VMEM((TB, 8, TB), jnp.bfloat16),
            pltpu.VMEM((PARTS, TB, CHUNK, TB), jnp.bfloat16),
            pltpu.VMEM((1024, 2 * TB), jnp.float32),
            pltpu.VMEM((2, 16 * TB, 2 * TB), jnp.bfloat16),
            pltpu.SemaphoreType.DMA,
            pltpu.SemaphoreType.DMA((PARTS,)),
        ],
        compiler_params=pltpu.CompilerParams(vmem_limit_bytes=VMEM_LIMIT),
        cost_estimate=pl.CostEstimate(flops=5_000_000_000, bytes_accessed=5_000_000, transcendentals=0),
    )(arrived)


def body(blocks, dest, slot, template, kern_rows, kern_cols, coeffs):
    parcels = turned(blocks, dest, slot)
    arrived = lax.all_to_all(parcels, AXES, split_axis=0, concat_axis=0, tiled=True)
    sums, keys, blank = merged(arrived)
    model = model_of(with_halo(template, blank), kern_rows, kern_cols, coeffs)
    gathered = lax.all_to_all(sums, AXES, split_axis=0, concat_axis=0, tiled=True)
    mine = lax.axis_index("col") * 4 + lax.axis_index("row")
    tiles = (mine * 16 + jnp.arange(16, dtype=jnp.int32)).astype(jnp.float32)
    counts = (keys[None] == tiles[:, None, None]).astype(jnp.float32).sum(axis=(1, 2))
    inverse = 1.0 / jnp.maximum(counts, 1.0)
    science = (
        (gathered.astype(jnp.float32) * inverse[None, :, None])
        .reshape(TB, GRID, GRID, TB)
        .transpose(1, 0, 2, 3)
        .reshape(EXTENT, EXTENT)
    )
    return (science - model).astype(jnp.bfloat16)


def solution(mesh):
    placed = (P(AXES, None, None), P(AXES, None), P(AXES), P("row", "col"), P(), P(), P())
    return jax.shard_map(body, mesh=mesh, in_specs=placed, out_specs=P("row", "col"), check_vma=False)
```

```python
import functools

import jax
import jax.numpy as jnp
from jax import lax
from jax.experimental import pallas as pl
from jax.experimental.pallas import tpu as pltpu
from jax.sharding import PartitionSpec as P

HALF = 15
TAPS = 31
BASES = 9
GRID = 4
TB = 128
EXTENT = GRID * TB
AXES = ("col", "row")
CHUNK = 16
PARTS = TB // CHUNK
DEPTH = 512
VMEM_LIMIT = 56 << 20


def edge_shift(cells, axis, up):
    count = lax.axis_size(axis)
    if up:
        pairs = [(i, i + 1) for i in range(count - 1)]
    else:
        pairs = [(i + 1, i) for i in range(count - 1)]
    return lax.ppermute(cells, axis, pairs)


def with_halo(template, blank):
    left = edge_shift(template[:, EXTENT - HALF:], "col", True)
    right = edge_shift(template[:, :HALF], "col", False)
    wide = jnp.concatenate([left, template, right], axis=1)
    above = edge_shift(wide[EXTENT - HALF:], "row", True)
    below = edge_shift(wide[:HALF], "row", False)
    tall = jnp.concatenate([above, wide, below], axis=0)
    return (jnp.pad(tall, ((0, 2), (0, 98))).astype(jnp.float32) + blank).astype(jnp.bfloat16)


def toeplitz(taps_row):
    spread = jnp.broadcast_to(taps_row, (TB, 2 * TB))
    return pltpu.roll(spread, 0, 1, stride=1, stride_axis=0).astype(jnp.bfloat16)


def model_kernel(coeffs_ref, origin_ref, padded_ref, rows_ref, cols_ref, model_ref, band_rows, band_cols, passed):
    for b in range(BASES):
        band_rows[b * TB:(b + 1) * TB, :] = toeplitz(rows_ref[b:b + 1, :])
        band_cols[b] = toeplitz(cols_ref[b:b + 1, :])
    height_all = float(EXTENT * 4)
    width_all = float(EXTENT * 32)
    for q in range(GRID):
        stacked = jnp.dot(
            band_rows[:, :160], padded_ref[q * TB:q * TB + 160, :], preferred_element_type=jnp.float32
        ).astype(jnp.bfloat16)
        for b in range(BASES):
            passed[b, q * TB:(q + 1) * TB, :] = stacked[b * TB:(b + 1) * TB, :]
    local_y = lax.broadcasted_iota(jnp.int32, (EXTENT, TB), 0)
    coord_y = 2.0 * (local_y.astype(jnp.float32) + (origin_ref[0] + 0.5)) / height_all - 1.0
    for p in range(GRID):
        local_x = lax.broadcasted_iota(jnp.int32, (1, TB), 1) + p * TB
        coord_x = 2.0 * (local_x.astype(jnp.float32) + (origin_ref[1] + 0.5)) / width_all - 1.0
        total = jnp.zeros((EXTENT, TB), jnp.float32)
        for b in range(BASES):
            image = lax.dot_general(
                passed[b, :, p * TB:(p + 2) * TB],
                band_cols[b],
                (((1,), (1,)), ((), ())),
                preferred_element_type=jnp.float32,
            )
            weight = (coeffs_ref[3 * b] + coeffs_ref[3 * b + 1] * coord_x) + coeffs_ref[3 * b + 2] * coord_y
            total = total + weight * image
        model_ref[:, p * TB:(p + 1) * TB] = total


def model_of(padded, kern_rows, kern_cols, coeffs):
    taps_rows = jnp.pad(kern_rows.astype(jnp.float32), ((0, 7), (0, 2 * TB - TAPS)))
    taps_cols = jnp.pad(kern_cols.astype(jnp.float32), ((0, 7), (0, 2 * TB - TAPS)))
    origin = jnp.stack([
        lax.axis_index("row").astype(jnp.float32) * EXTENT,
        lax.axis_index("col").astype(jnp.float32) * EXTENT,
    ])
    smem = pl.BlockSpec(memory_space=pltpu.SMEM)
    vmem = pl.BlockSpec(memory_space=pltpu.VMEM)
    return pl.pallas_call(
        model_kernel,
        out_shape=jax.ShapeDtypeStruct((EXTENT, EXTENT), jnp.float32),
        in_specs=[smem, smem, vmem, vmem, vmem],
        out_specs=vmem,
        scratch_shapes=[
            pltpu.VMEM((BASES * TB, 2 * TB), jnp.bfloat16),
            pltpu.VMEM((BASES, TB, 2 * TB), jnp.bfloat16),
            pltpu.VMEM((BASES, EXTENT, 640), jnp.bfloat16),
        ],
        compiler_params=pltpu.CompilerParams(vmem_limit_bytes=32 << 20),
        cost_estimate=pl.CostEstimate(flops=3_000_000_000, bytes_accessed=2_000_000, transcendentals=0),
    )(coeffs.reshape(-1), origin, padded, taps_rows, taps_cols)


def turn_kernel(dest_ref, slot_ref, blocks_ref, out_ref, loaded, swapped, ready, arriving, leaving):
    arrivals = []
    for k in range(PARTS):
        part = pl.ds(k * CHUNK, CHUNK)
        arrivals.append(pltpu.make_async_copy(blocks_ref.at[part], loaded.at[part], arriving.at[k]))
        arrivals[k].start()
    dests = dest_ref[...].astype(jnp.float32)
    slots = slot_ref[...].astype(jnp.float32)
    ranked = dests * float(TB) + lax.broadcasted_iota(jnp.int32, (1, TB), 1).astype(jnp.float32)
    across = jnp.broadcast_to(ranked, (TB, TB))
    place = jnp.where(across.T < across, 1.0, 0.0).sum(axis=0, keepdims=True)
    down = lax.broadcasted_iota(jnp.int32, (TB, TB), 0).astype(jnp.float32)
    order = jnp.where(down == place, 1.0, 0.0).astype(jnp.bfloat16)
    pair = jnp.concatenate([dests, slots, jnp.zeros((14, TB), jnp.float32)], axis=0).astype(jnp.bfloat16)
    labels = lax.dot_general(
        pair, order, (((1,), (1,)), ((), ())), preferred_element_type=jnp.float32
    ).astype(jnp.bfloat16)[:8]
    for k in range(PARTS):
        arrivals[k].wait()
        part = pl.ds(k * CHUNK, CHUNK)
        swapped[:, part, :] = jnp.swapaxes(loaded[part], 0, 1)
    departures = []
    for k in range(PARTS):
        for r in range(k * CHUNK, (k + 1) * CHUNK):
            ready[r, :TB, :] = jnp.dot(
                order, swapped[r], preferred_element_type=jnp.float32
            ).astype(jnp.bfloat16)
            ready[r, TB:, :] = labels
        part = pl.ds(k * CHUNK, CHUNK)
        departures.append(pltpu.make_async_copy(ready.at[part], out_ref.at[part], leaving.at[k]))
        departures[k].start()
    for k in range(PARTS):
        departures[k].wait()


def turned(blocks, dest, slot):
    label = pl.BlockSpec(memory_space=pltpu.VMEM)
    far = pl.BlockSpec(memory_space=pl.ANY)
    return pl.pallas_call(
        turn_kernel,
        out_shape=jax.ShapeDtypeStruct((TB, TB + 8, TB), jnp.bfloat16),
        in_specs=[label, label, far],
        out_specs=far,
        scratch_shapes=[
            pltpu.VMEM((TB, TB, TB), jnp.bfloat16),
            pltpu.VMEM((TB, TB, TB), jnp.bfloat16),
            pltpu.VMEM((TB, TB + 8, TB), jnp.bfloat16),
            pltpu.SemaphoreType.DMA((PARTS,)),
            pltpu.SemaphoreType.DMA((PARTS,)),
        ],
        compiler_params=pltpu.CompilerParams(vmem_limit_bytes=VMEM_LIMIT),
        cost_estimate=pl.CostEstimate(flops=600_000_000, bytes_accessed=8_700_000, transcendentals=0),
    )(dest.reshape(1, TB), slot.reshape(1, TB), blocks)


def merge_kernel(arrived_ref, out_ref, keys_ref, blank_ref, labels, rows, acc, spread, labels_sem, rows_sem):
    named = pltpu.make_async_copy(arrived_ref.at[:, pl.ds(TB, 8), :], labels, labels_sem)
    named.start()
    arrivals = []
    for k in range(PARTS):
        part = pl.ds(k * CHUNK, CHUNK)
        arrivals.append(pltpu.make_async_copy(arrived_ref.at[:, part, :], rows.at[k], rows_sem.at[k]))
        arrivals[k].start()
    acc[...] = jnp.zeros_like(acc)
    lanes = lax.broadcasted_iota(jnp.int32, (TB, TB), 1) // CHUNK
    owners = lax.broadcasted_iota(jnp.int32, (TB, TB), 0) % 8
    named.wait()
    tags = labels[...].astype(jnp.float32)
    keys = tags[:, 0, :] * 16.0 + tags[:, 1, :]
    keys_ref[...] = keys
    blank_ref[...] = jnp.zeros_like(blank_ref)
    skewed = pltpu.roll(keys, 0, 1, stride=CHUNK, stride_axis=0)
    for k in range(PARTS):
        arrivals[k].wait()
    for k in range(PARTS):
        shifted = pltpu.roll(skewed, (TB - k * CHUNK) % TB, 1)
        lines = jnp.where(lanes == owners, shifted, 0.0).reshape(16, 8, TB).sum(axis=1)
        dests = jnp.floor(lines * (1.0 / 16.0))
        slots = lines - 16.0 * dests
        high = jnp.where(slots >= 8.0, 1.0, 0.0)
        places = dests * 8.0 + slots - 8.0 * high - float(k * 64)
        high_down = high.T
        for g in range(16):
            taken = rows[k, g * 8:(g + 1) * 8].reshape(TB, TB)
            mask = jnp.broadcast_to(high_down[:, g:g + 1], (TB, TB)).astype(jnp.bfloat16)
            upper = taken * mask
            spread[k % 4, g * TB:(g + 1) * TB, TB:] = upper
            spread[k % 4, g * TB:(g + 1) * TB, :TB] = taken - upper
        line = jnp.concatenate([places[g:g + 1, :] for g in range(16)], axis=1)
        for first, size in ((0, 320), (320, 256)):
            middle = size // 2
            marks = (lax.broadcasted_iota(jnp.int32, (size, DEPTH), 0) - middle).astype(jnp.bfloat16)
            wanted = (line - float(first + middle)).astype(jnp.bfloat16)
            window = slice(k * 64 + first, k * 64 + first + size)
            total = acc[window, :]
            for q in range(0, 16 * TB, DEPTH):
                chosen = jnp.where(marks == wanted[:, q:q + DEPTH], jnp.bfloat16(1), jnp.bfloat16(0))
                total = total + jnp.dot(chosen, spread[k % 4, q:q + DEPTH, :], preferred_element_type=jnp.float32)
            acc[window, :] = total
    whole = acc[...].reshape(TB, 8, 2 * TB)
    out_ref[...] = jnp.concatenate([whole[:, :, :TB], whole[:, :, TB:]], axis=1).astype(jnp.bfloat16)


def merged(arrived):
    near = pl.BlockSpec(memory_space=pltpu.VMEM)
    return pl.pallas_call(
        merge_kernel,
        out_shape=(
            jax.ShapeDtypeStruct((TB, 16, TB), jnp.bfloat16),
            jax.ShapeDtypeStruct((TB, TB), jnp.float32),
            jax.ShapeDtypeStruct((1, 640), jnp.float32),
        ),
        in_specs=[pl.BlockSpec(memory_space=pl.ANY)],
        out_specs=(near, near, near),
        scratch_shapes=[
            pltpu.VMEM((TB, 8, TB), jnp.bfloat16),
            pltpu.VMEM((PARTS, TB, CHUNK, TB), jnp.bfloat16),
            pltpu.VMEM((1024, 2 * TB), jnp.float32),
            pltpu.VMEM((4, 16 * TB, 2 * TB), jnp.bfloat16),
            pltpu.SemaphoreType.DMA,
            pltpu.SemaphoreType.DMA((PARTS,)),
        ],
        compiler_params=pltpu.CompilerParams(vmem_limit_bytes=VMEM_LIMIT),
        cost_estimate=pl.CostEstimate(flops=5_000_000_000, bytes_accessed=5_000_000, transcendentals=0),
    )(arrived)


def body(blocks, dest, slot, template, kern_rows, kern_cols, coeffs):
    parcels = turned(blocks, dest, slot)
    arrived = lax.all_to_all(parcels, AXES, split_axis=0, concat_axis=0, tiled=True)
    sums, keys, blank = merged(arrived)
    model = model_of(with_halo(template, blank), kern_rows, kern_cols, coeffs)
    gathered = lax.all_to_all(sums, AXES, split_axis=0, concat_axis=0, tiled=True)
    mine = lax.axis_index("col") * 4 + lax.axis_index("row")
    tiles = (mine * 16 + jnp.arange(16, dtype=jnp.int32)).astype(jnp.float32)
    counts = (keys[None] == tiles[:, None, None]).astype(jnp.float32).sum(axis=(1, 2))
    inverse = 1.0 / jnp.maximum(counts, 1.0)
    science = (
        (gathered.astype(jnp.float32) * inverse[None, :, None])
        .reshape(TB, GRID, GRID, TB)
        .transpose(1, 0, 2, 3)
        .reshape(EXTENT, EXTENT)
    )
    return (science - model).astype(jnp.bfloat16)


def solution(mesh):
    placed = (P(AXES, None, None), P(AXES, None), P(AXES), P("row", "col"), P(), P(), P())
    return jax.shard_map(body, mesh=mesh, in_specs=placed, out_specs=P("row", "col"), check_vma=False)
```

```python
import functools

import jax
import jax.numpy as jnp
from jax import lax
from jax.experimental import pallas as pl
from jax.experimental.pallas import tpu as pltpu
from jax.sharding import PartitionSpec as P

HALF = 15
TAPS = 31
BASES = 9
GRID = 4
TB = 128
EXTENT = GRID * TB
AXES = ("col", "row")
CHUNK = 16
PARTS = TB // CHUNK
DEPTH = 512
VMEM_LIMIT = 56 << 20


def edge_shift(cells, axis, up):
    count = lax.axis_size(axis)
    if up:
        pairs = [(i, i + 1) for i in range(count - 1)]
    else:
        pairs = [(i + 1, i) for i in range(count - 1)]
    return lax.ppermute(cells, axis, pairs)


def with_halo(template, blank):
    above = edge_shift(template[EXTENT - HALF:], "row", True)
    below = edge_shift(template[:HALF], "row", False)
    tall = jnp.concatenate([above, template, below], axis=0)
    left = edge_shift(tall[:, EXTENT - HALF:], "col", True)
    right = edge_shift(tall[:, :HALF], "col", False)
    tall = jnp.concatenate([left, tall, right], axis=1)
    return (jnp.pad(tall, ((0, 2), (0, 98))).astype(jnp.float32) + blank).astype(jnp.bfloat16)


def toeplitz(taps_row):
    spread = jnp.broadcast_to(taps_row, (TB, 2 * TB))
    return pltpu.roll(spread, 0, 1, stride=1, stride_axis=0).astype(jnp.bfloat16)


def model_kernel(coeffs_ref, origin_ref, padded_ref, rows_ref, cols_ref, model_ref, band_rows, band_cols, passed):
    for b in range(BASES):
        band_rows[b * TB:(b + 1) * TB, :] = toeplitz(rows_ref[b:b + 1, :])
        band_cols[b] = toeplitz(cols_ref[b:b + 1, :])
    height_all = float(EXTENT * 4)
    width_all = float(EXTENT * 32)
    for q in range(GRID):
        stacked = jnp.dot(
            band_rows[:, :160], padded_ref[q * TB:q * TB + 160, :], preferred_element_type=jnp.float32
        ).astype(jnp.bfloat16)
        for b in range(BASES):
            passed[b, q * TB:(q + 1) * TB, :] = stacked[b * TB:(b + 1) * TB, :]
    local_y = lax.broadcasted_iota(jnp.int32, (EXTENT, TB), 0)
    coord_y = 2.0 * (local_y.astype(jnp.float32) + (origin_ref[0] + 0.5)) / height_all - 1.0
    for p in range(GRID):
        local_x = lax.broadcasted_iota(jnp.int32, (1, TB), 1) + p * TB
        coord_x = 2.0 * (local_x.astype(jnp.float32) + (origin_ref[1] + 0.5)) / width_all - 1.0
        total = jnp.zeros((EXTENT, TB), jnp.float32)
        for b in range(BASES):
            image = lax.dot_general(
                passed[b, :, p * TB:(p + 2) * TB],
                band_cols[b],
                (((1,), (1,)), ((), ())),
                preferred_element_type=jnp.float32,
            )
            weight = (coeffs_ref[3 * b] + coeffs_ref[3 * b + 1] * coord_x) + coeffs_ref[3 * b + 2] * coord_y
            total = total + weight * image
        model_ref[:, p * TB:(p + 1) * TB] = total


def model_of(padded, kern_rows, kern_cols, coeffs):
    taps_rows = jnp.pad(kern_rows.astype(jnp.float32), ((0, 7), (0, 2 * TB - TAPS)))
    taps_cols = jnp.pad(kern_cols.astype(jnp.float32), ((0, 7), (0, 2 * TB - TAPS)))
    origin = jnp.stack([
        lax.axis_index("row").astype(jnp.float32) * EXTENT,
        lax.axis_index("col").astype(jnp.float32) * EXTENT,
    ])
    smem = pl.BlockSpec(memory_space=pltpu.SMEM)
    vmem = pl.BlockSpec(memory_space=pltpu.VMEM)
    return pl.pallas_call(
        model_kernel,
        out_shape=jax.ShapeDtypeStruct((EXTENT, EXTENT), jnp.float32),
        in_specs=[smem, smem, vmem, vmem, vmem],
        out_specs=vmem,
        scratch_shapes=[
            pltpu.VMEM((BASES * TB, 2 * TB), jnp.bfloat16),
            pltpu.VMEM((BASES, TB, 2 * TB), jnp.bfloat16),
            pltpu.VMEM((BASES, EXTENT, 640), jnp.bfloat16),
        ],
        compiler_params=pltpu.CompilerParams(vmem_limit_bytes=32 << 20),
        cost_estimate=pl.CostEstimate(flops=3_000_000_000, bytes_accessed=2_000_000, transcendentals=0),
    )(coeffs.reshape(-1), origin, padded, taps_rows, taps_cols)


def turn_kernel(dest_ref, slot_ref, blocks_ref, out_ref, loaded, swapped, ready, arriving, leaving):
    arrivals = []
    for k in range(PARTS):
        part = pl.ds(k * CHUNK, CHUNK)
        arrivals.append(pltpu.make_async_copy(blocks_ref.at[part], loaded.at[part], arriving.at[k]))
        arrivals[k].start()
    dests = dest_ref[...].astype(jnp.float32)
    slots = slot_ref[...].astype(jnp.float32)
    ranked = dests * float(TB) + lax.broadcasted_iota(jnp.int32, (1, TB), 1).astype(jnp.float32)
    across = jnp.broadcast_to(ranked, (TB, TB))
    place = jnp.where(across.T < across, 1.0, 0.0).sum(axis=0, keepdims=True)
    down = lax.broadcasted_iota(jnp.int32, (TB, TB), 0).astype(jnp.float32)
    order = jnp.where(down == place, 1.0, 0.0).astype(jnp.bfloat16)
    pair = jnp.concatenate([dests, slots, jnp.zeros((14, TB), jnp.float32)], axis=0).astype(jnp.bfloat16)
    labels = lax.dot_general(
        pair, order, (((1,), (1,)), ((), ())), preferred_element_type=jnp.float32
    ).astype(jnp.bfloat16)[:8]
    for k in range(PARTS):
        arrivals[k].wait()
        part = pl.ds(k * CHUNK, CHUNK)
        swapped[:, part, :] = jnp.swapaxes(loaded[part], 0, 1)
    departures = []
    for k in range(PARTS):
        for r in range(k * CHUNK, (k + 1) * CHUNK):
            ready[r, :TB, :] = jnp.dot(
                order, swapped[r], preferred_element_type=jnp.float32
            ).astype(jnp.bfloat16)
            ready[r, TB:, :] = labels
        part = pl.ds(k * CHUNK, CHUNK)
        departures.append(pltpu.make_async_copy(ready.at[part], out_ref.at[part], leaving.at[k]))
        departures[k].start()
    for k in range(PARTS):
        departures[k].wait()


def turned(blocks, dest, slot):
    label = pl.BlockSpec(memory_space=pltpu.VMEM)
    far = pl.BlockSpec(memory_space=pl.ANY)
    return pl.pallas_call(
        turn_kernel,
        out_shape=jax.ShapeDtypeStruct((TB, TB + 8, TB), jnp.bfloat16),
        in_specs=[label, label, far],
        out_specs=far,
        scratch_shapes=[
            pltpu.VMEM((TB, TB, TB), jnp.bfloat16),
            pltpu.VMEM((TB, TB, TB), jnp.bfloat16),
            pltpu.VMEM((TB, TB + 8, TB), jnp.bfloat16),
            pltpu.SemaphoreType.DMA((PARTS,)),
            pltpu.SemaphoreType.DMA((PARTS,)),
        ],
        compiler_params=pltpu.CompilerParams(vmem_limit_bytes=VMEM_LIMIT),
        cost_estimate=pl.CostEstimate(flops=600_000_000, bytes_accessed=8_700_000, transcendentals=0),
    )(dest.reshape(1, TB), slot.reshape(1, TB), blocks)


def merge_kernel(arrived_ref, out_ref, keys_ref, blank_ref, labels, rows, acc, spread, labels_sem, rows_sem):
    named = pltpu.make_async_copy(arrived_ref.at[:, pl.ds(TB, 8), :], labels, labels_sem)
    named.start()
    arrivals = []
    for k in range(PARTS):
        part = pl.ds(k * CHUNK, CHUNK)
        arrivals.append(pltpu.make_async_copy(arrived_ref.at[:, part, :], rows.at[k], rows_sem.at[k]))
        arrivals[k].start()
    acc[...] = jnp.zeros_like(acc)
    lanes = lax.broadcasted_iota(jnp.int32, (TB, TB), 1) // CHUNK
    owners = lax.broadcasted_iota(jnp.int32, (TB, TB), 0) % 8
    named.wait()
    tags = labels[...].astype(jnp.float32)
    keys = tags[:, 0, :] * 16.0 + tags[:, 1, :]
    keys_ref[...] = keys
    blank_ref[...] = jnp.zeros_like(blank_ref)
    skewed = pltpu.roll(keys, 0, 1, stride=CHUNK, stride_axis=0)
    for k in range(PARTS):
        arrivals[k].wait()
    for k in range(PARTS):
        shifted = pltpu.roll(skewed, (TB - k * CHUNK) % TB, 1)
        lines = jnp.where(lanes == owners, shifted, 0.0).reshape(16, 8, TB).sum(axis=1)
        dests = jnp.floor(lines * (1.0 / 16.0))
        slots = lines - 16.0 * dests
        high = jnp.where(slots >= 8.0, 1.0, 0.0)
        places = dests * 8.0 + slots - 8.0 * high - float(k * 64)
        high_down = high.T
        for g in range(16):
            taken = rows[k, g * 8:(g + 1) * 8].reshape(TB, TB)
            mask = jnp.broadcast_to(high_down[:, g:g + 1], (TB, TB)).astype(jnp.bfloat16)
            upper = taken * mask
            spread[k % 2, g * TB:(g + 1) * TB, TB:] = upper
            spread[k % 2, g * TB:(g + 1) * TB, :TB] = taken - upper
        line = jnp.concatenate([places[g:g + 1, :] for g in range(16)], axis=1)
        for first, size in ((0, 256), (256, 320)):
            middle = size // 2
            marks = (lax.broadcasted_iota(jnp.int32, (size, DEPTH), 0) - middle).astype(jnp.bfloat16)
            wanted = (line - float(first + middle)).astype(jnp.bfloat16)
            window = slice(k * 64 + first, k * 64 + first + size)
            total = acc[window, :]
            for q in range(0, 16 * TB, DEPTH):
                chosen = jnp.where(marks == wanted[:, q:q + DEPTH], jnp.bfloat16(1), jnp.bfloat16(0))
                total = total + jnp.dot(chosen, spread[k % 2, q:q + DEPTH, :], preferred_element_type=jnp.float32)
            acc[window, :] = total
    whole = acc[...].reshape(TB, 8, 2 * TB)
    out_ref[...] = jnp.concatenate([whole[:, :, :TB], whole[:, :, TB:]], axis=1).astype(jnp.bfloat16)


def merged(arrived):
    near = pl.BlockSpec(memory_space=pltpu.VMEM)
    return pl.pallas_call(
        merge_kernel,
        out_shape=(
            jax.ShapeDtypeStruct((TB, 16, TB), jnp.bfloat16),
            jax.ShapeDtypeStruct((TB, TB), jnp.float32),
            jax.ShapeDtypeStruct((1, 640), jnp.float32),
        ),
        in_specs=[pl.BlockSpec(memory_space=pl.ANY)],
        out_specs=(near, near, near),
        scratch_shapes=[
            pltpu.VMEM((TB, 8, TB), jnp.bfloat16),
            pltpu.VMEM((PARTS, TB, CHUNK, TB), jnp.bfloat16),
            pltpu.VMEM((1024, 2 * TB), jnp.float32),
            pltpu.VMEM((2, 16 * TB, 2 * TB), jnp.bfloat16),
            pltpu.SemaphoreType.DMA,
            pltpu.SemaphoreType.DMA((PARTS,)),
        ],
        compiler_params=pltpu.CompilerParams(vmem_limit_bytes=VMEM_LIMIT),
        cost_estimate=pl.CostEstimate(flops=5_000_000_000, bytes_accessed=5_000_000, transcendentals=0),
    )(arrived)


def body(blocks, dest, slot, template, kern_rows, kern_cols, coeffs):
    parcels = turned(blocks, dest, slot)
    arrived = lax.all_to_all(parcels, AXES, split_axis=0, concat_axis=0, tiled=True)
    sums, keys, blank = merged(arrived)
    model = model_of(with_halo(template, blank), kern_rows, kern_cols, coeffs)
    gathered = lax.all_to_all(sums, AXES, split_axis=0, concat_axis=0, tiled=True)
    mine = lax.axis_index("col") * 4 + lax.axis_index("row")
    tiles = (mine * 16 + jnp.arange(16, dtype=jnp.int32)).astype(jnp.float32)
    counts = (keys[None] == tiles[:, None, None]).astype(jnp.float32).sum(axis=(1, 2))
    inverse = 1.0 / jnp.maximum(counts, 1.0)
    science = (
        (gathered.astype(jnp.float32) * inverse[None, :, None])
        .reshape(TB, GRID, GRID, TB)
        .transpose(1, 0, 2, 3)
        .reshape(EXTENT, EXTENT)
    )
    return (science - model).astype(jnp.bfloat16)


def solution(mesh):
    placed = (P(AXES, None, None), P(AXES, None), P(AXES), P("row", "col"), P(), P(), P())
    return jax.shard_map(body, mesh=mesh, in_specs=placed, out_specs=P("row", "col"), check_vma=False)
```
